512 devices in a mesh: outer: 16 (over z_lo, core), inner: 32 (over x, z_hi, y).
Axes of the slice: x: 4, y: 4, z: 16 (z_hi: 2, z_lo: 8; z = z_hi * 8 + z_lo), core: 2. Of those that a mesh axis runs over, the one named last changes fastest.
Arguments:
- q_heads: bfloat16 [16, 4096, 1024], P('outer', 'inner'), may hold values from -6 to 6
- k_head: bfloat16 [16, 4096, 128], P('outer', 'inner'), may hold values from -6 to 6
- v_head: bfloat16 [16, 4096, 128], P('outer', 'inner'), may hold values from -6 to 6
- out_grad: bfloat16 [16, 4096, 1024], P('outer', 'inner'), may hold values from -6 to 6
- weight_codes: int32 [16, 4096], P('outer', 'inner'), may hold values from 1 to 16
- bounds: int32 [16, 2], P('outer'), may hold values from 1024 to 3071, as said below
- block_order: int32 [64], replicated, may hold values from 0 to 63, each once
Outputs:
- q_grad: bfloat16 [16, 4096, 1024], P('outer', 'inner')
- k_grad: bfloat16 [16, 4096, 128], P('outer', 'inner')
- v_grad: bfloat16 [16, 4096, 128], P('outer', 'inner')
- bias_grad: float32 [1280], replicated
The draws below stay inside these ranges and needn't reach their ends.
Inputs may be any that keep to these rules, and one draw needn't show every extreme that they name: `block_order`: a permutation: each value once. `bounds`: first column in [1024, 2048), second in [2048, 3072).
All inputs are finite; a program needn't handle non-finite values.
Results may differ from the reference program's by a relative error of at most 0.02.
Values may be sent and summed in bfloat16 or wider, within the bound.
A program may use at most 64 MiB of HBM per device.

```python
import math
import jax
import jax.numpy as jnp
from jax import lax

G = 8
DH = 128
TOK_DEV = 128
SEQ = 4096
PAIRS = 16
N_INNER = 32


def draw_q_heads(key, part):
    key = jax.random.fold_in(key, 1)
    base = jax.random.normal(key, (PAIRS, SEQ, G, DH), jnp.float32)
    base = jnp.clip(base, -6.0, 6.0)
    return base.reshape(PAIRS, SEQ, G * DH).astype(jnp.bfloat16)


def draw_k_head(key, part):
    key = jax.random.fold_in(key, 2)
    base = jax.random.normal(key, (PAIRS, SEQ, DH), jnp.float32)
    base = jnp.clip(base, -6.0, 6.0)
    return base.astype(jnp.bfloat16)


def draw_bounds(key, part):
    key = jax.random.fold_in(key, 3)
    opening = jax.random.randint(jax.random.fold_in(key, 1), (PAIRS, 1), SEQ // 4, SEQ // 2)
    closing = jax.random.randint(jax.random.fold_in(key, 2), (PAIRS, 1), SEQ // 2, 3 * SEQ // 4)
    chosen = jax.random.randint(jax.random.fold_in(key, 4), (), 0, PAIRS)
    marked = (jnp.arange(PAIRS) == chosen)[:, None]
    opening = jnp.where(marked, SEQ // 4, opening)
    closing = jnp.where(marked, 3 * SEQ // 4 - 1, closing)
    return jnp.concatenate([opening, closing], axis=1).astype(jnp.int32)


def set_ends(values, rng, least, high):
    extent = values.shape
    spot = [jax.random.randint(jax.random.fold_in(rng, axis), (), 0, extent[axis]) for axis in range(len(extent))]
    values = values.at[tuple(spot)].set(least)
    longest = extent.index(max(extent))
    spot[longest] = (spot[longest] + 1) % extent[longest]
    return values.at[tuple(spot)].set(high)


def shard_levels(own_key, dims, pieces, least, high):
    def one(dim, blocks):
        steps = jax.random.uniform(jax.random.fold_in(jax.random.fold_in(own_key, 6), dim), (blocks,), jnp.float32, least / len(pieces), high / len(pieces))
        return jnp.repeat(jnp.exp(steps), dims[dim] // blocks).reshape((-1,) + (1,) * (len(dims) - dim - 1))

    level = one(*pieces[0])
    for cut in pieces[1:]:
        level = level * one(*cut)
    return level


def noise(rng, shape, width, bound, cuts=(), held_as=jnp.bfloat16):
    values = width * jax.random.normal(rng, shape, jnp.float32)
    if cuts:
        values = values * shard_levels(rng, shape, cuts, -0.22, 0.18)
    return jnp.clip(values, -bound, bound).astype(held_as)


def setup_inputs(seed: int = 0) -> dict:
    streams_of = jax.random.split(jax.random.key(seed), 8)
    q_heads = draw_q_heads(jax.random.fold_in(streams_of[7], 71), 0)
    k_head = draw_k_head(jax.random.fold_in(streams_of[7], 71), 0)
    v_head = noise(streams_of[2], (PAIRS, SEQ, DH), 1.0, 6.0, ((0, 16), (1, 32)))
    out_grad = noise(streams_of[3], (PAIRS, SEQ, G * DH), 1.0, 6.0, ((0, 16), (1, 32)))
    weight_codes = set_ends(jax.random.randint(streams_of[4], (PAIRS, SEQ), 1, 17), jax.random.fold_in(streams_of[4], 1), 1, 16).astype(jnp.int32)
    bounds = draw_bounds(jax.random.fold_in(streams_of[7], 71), 0)
    block_order = jax.random.permutation(streams_of[6], 2 * N_INNER).astype(jnp.int32)
    return dict(q_heads=q_heads, k_head=k_head, v_head=v_head, out_grad=out_grad, weight_codes=weight_codes, bounds=bounds, block_order=block_order)


NEG_SCORE = -1e+30

def visible(q_pos, k_pos, pair_start, second_start):
    later = q_pos[:, None] >= k_pos[None, :]
    crossed = (k_pos[None, :] >= pair_start) & (k_pos[None, :] < second_start) & (q_pos[:, None] >= second_start)
    return later & jnp.logical_not(crossed)

def one_pair(q_heads, k_head, v_head, out_grad, weight_codes, bounds, position):
    seq_len = k_head.shape[0]
    head_width = k_head.shape[1]
    head_count = q_heads.shape[1] // head_width
    inv_scale = 1.0 / math.sqrt(head_width)
    block_rows = min(512, seq_len)
    queries = q_heads.reshape(seq_len, head_count, head_width).astype(jnp.float32)
    weighted_low = (out_grad.astype(jnp.float32) * (weight_codes.astype(jnp.float32) / 16.0)[:, None]).astype(jnp.bfloat16)
    weighted = lax.optimization_barrier(weighted_low).astype(jnp.float32).reshape(seq_len, head_count, head_width)
    keys_full = k_head.astype(jnp.float32)
    vals_full = v_head.astype(jnp.float32)
    pair_start = bounds[0]
    second_start = bounds[1]

    def block_step(carry, block_index):
        k_acc, v_acc = carry
        start = (block_index * block_rows).astype(jnp.int32)
        q_block = lax.dynamic_slice_in_dim(queries, start, block_rows, 0)
        g_block = lax.dynamic_slice_in_dim(weighted, start, block_rows, 0)
        q_pos = lax.dynamic_slice_in_dim(position, start, block_rows, 0)
        allowed = visible(q_pos, position, pair_start, second_start)[None]
        scores = jnp.einsum('qhd,kd->hqk', q_block, keys_full) * inv_scale
        largest = lax.optimization_barrier(jnp.max(jnp.where(allowed, scores, NEG_SCORE), axis=2))
        totals = lax.optimization_barrier(jnp.sum(jnp.where(allowed, jnp.exp(scores - largest[:, :, None]), 0.0), axis=2))
        log_total = largest + jnp.log(totals)
        probs = jnp.where(allowed, jnp.exp(scores - log_total[:, :, None]), 0.0)
        probs_low = lax.optimization_barrier(probs.astype(jnp.bfloat16)).astype(jnp.float32)
        attn_out = jnp.einsum('hqk,kd->qhd', probs, vals_full)
        delta = lax.optimization_barrier(jnp.sum(g_block * attn_out, axis=2))
        dprobs = jnp.einsum('qhd,kd->hqk', g_block, vals_full)
        dscores = probs * (dprobs - delta.T[:, :, None])
        dscores_low = lax.optimization_barrier(dscores.astype(jnp.bfloat16)).astype(jnp.float32)
        q_part = jnp.einsum('hqk,kd->qhd', dscores_low, keys_full) * inv_scale
        k_acc = k_acc + jnp.einsum('hqk,qhd->kd', dscores_low, q_block) * inv_scale
        v_acc = v_acc + jnp.einsum('hqk,qhd->kd', probs_low, g_block)
        return ((k_acc, v_acc), q_part)
    zeros_kv = jnp.zeros((seq_len, head_width), jnp.float32)
    (k_full, v_full), q_parts = lax.scan(block_step, (zeros_kv, zeros_kv), jnp.arange(seq_len // block_rows, dtype=jnp.int32))
    q_full = q_parts.reshape(seq_len, head_count * head_width)
    return (q_full, k_full, v_full)

def reference(q_heads, k_head, v_head, out_grad, weight_codes, bounds, block_order):
    half_rows = TOK_DEV // 2
    position = (block_order[:, None] * half_rows + jnp.arange(half_rows, dtype=jnp.int32)[None, :]).reshape(-1).astype(jnp.int32)

    def per_pair(items):
        return one_pair(items[0], items[1], items[2], items[3], items[4], items[5], position)
    q_full, k_full, v_full = lax.map(per_pair, (q_heads, k_head, v_head, out_grad, weight_codes, bounds))
    sums = jnp.concatenate([lax.optimization_barrier(jnp.sum(q_full, axis=(0, 1))), lax.optimization_barrier(jnp.sum(k_full, axis=(0, 1))), lax.optimization_barrier(jnp.sum(v_full, axis=(0, 1)))])
    bias_grad = sums / math.sqrt(PAIRS * SEQ)
    return (q_full.astype(jnp.bfloat16), k_full.astype(jnp.bfloat16), v_full.astype(jnp.bfloat16), bias_grad)
```

```python
import functools
import math

import jax
import jax.numpy as jnp
from jax import lax
from jax.experimental import pallas as pl
from jax.experimental.pallas import tpu as pltpu
from jax.sharding import PartitionSpec as P

MESH = pl.DeviceIdType.MESH
BF = jnp.bfloat16
F32 = jnp.float32
HEADS = 8
DH = 128
TOK = 128
HALF = 64
ROWS = HEADS * TOK
UNIT = 4 * TOK
SCALE = 1.0 / math.sqrt(DH)
LOG2E_SCALE = math.log2(math.e) / math.sqrt(DH)
MASKED = -(2.0**99)


class Place:
    def __init__(self):
        outer = lax.axis_index("outer")
        inner = lax.axis_index("inner")
        self.inner = inner
        self.core = outer % 2
        self.x = inner // 8
        self.y = inner % 4
        self.z = (inner // 4) % 2 * 8 + outer // 2
        self.a = self.x + self.core * (self.y - self.x)
        self.b = self.y + self.core * (self.x - self.y)

    def at(self, x, y, z, core):
        return (z % 8 * 2 + core, (x * 2 + z // 8) * 4 + y)

    def near(self, da, db, dz=0):
        a = (self.a + da) % 4
        b = (self.b + db) % 4
        x = a + self.core * (b - a)
        y = b + self.core * (a - b)
        return self.at(x, y, (self.z + dz) % 16, self.core)

    def in_plane(self, slot):
        return self.at(slot // 4, slot % 4, self.z, self.core)

    def along_z(self, z):
        return self.at(self.x, self.y, z, self.core)

    def other_core(self):
        return self.at(self.x, self.y, self.z, 1 - self.core)


def remote(src, dst, send_sem, recv_sem, device):
    return pltpu.make_async_remote_copy(
        src_ref=src,
        dst_ref=dst,
        send_sem=send_sem,
        recv_sem=recv_sem,
        device_id=device,
        device_id_type=MESH,
    )


def kernel(
    q_hbm, k_ref, v_ref, g_hbm, w_ref, bounds_ref, order_ref,
    dq_ref, dk_ref, dv_ref, bias_ref,
    q_in, g_in, kv, feat, qt, gt, q_rows, g_rows, kt, diag,
    e_all, dp_all, m_all, m_run, l_run, d_run, dq_t,
    part, got_b, line, got_a, fin, got_z, sum_kv,
    own_sum, plane_sums, plane_sum, z_sums, z_sum, core_sums,
    in_sem, gather_send, gather_recv, b_send, b_recv, a_send, a_recv, z_sem,
    plane_send, plane_recv, zs_send, zs_recv, core_sem,
):
    me = Place()
    slot = me.x * 4 + me.y
    q_copy = pltpu.make_async_copy(q_hbm.at[0], q_in, in_sem.at[0])
    g_copy = pltpu.make_async_copy(g_hbm.at[0], g_in, in_sem.at[1])
    q_copy.start()
    g_copy.start()

    barrier = pltpu.get_barrier_semaphore()

    def greet(j, carry):
        for device in (me.in_plane((slot + j) % 16), me.along_z((me.z + j) % 16)):
            pl.semaphore_signal(barrier, inc=1, device_id=device, device_id_type=MESH)
        return carry

    lax.fori_loop(1, 16, greet, 0)
    pl.semaphore_signal(barrier, inc=1, device_id=me.other_core(), device_id_type=MESH)
    kv[0, 0, 0, 0] = k_ref[0]
    kv[0, 0, 0, 1] = v_ref[0]
    pl.semaphore_wait(barrier, 31)

    def block(p, s, r, source, device):
        return remote(
            kv.at[source], kv.at[p, s, r], gather_send.at[p, s, r], gather_recv.at[p, s, r], device
        )

    def along_a(p, r):
        return block(p, 0, r, (p, 0, 0), me.near(r, 0))

    def along_b(p, s, r):
        return block(p, s, r, (p, 0, r), me.near(0, s))

    def across():
        return block(1, 0, 0, (0, 0, 0), me.near(0, 0, 8))

    def open_plane(p):
        for r in (2, 1, 3):
            along_a(p, r).start()
        for s in (2, 1, 3):
            along_b(p, s, 0).start()

    def spread_plane(p):
        for r in (1, 3, 2):
            along_a(p, r).wait_recv()
            for s in (2, 1, 3):
                along_b(p, s, r).start()

    across().start()
    open_plane(0)

    pair_start = bounds_ref[0, 0]
    second_start = bounds_ref[0, 1]
    lane = lax.broadcasted_iota(jnp.int32, (TOK, TOK), 1)
    sub = lax.broadcasted_iota(jnp.int32, (TOK, TOK), 0)
    first = order_ref[2 * me.inner]
    second = order_ref[2 * me.inner + 1]
    lane_block = jnp.where(lane < HALF, first, second)
    lane_pos = lane_block * HALF + lane % HALF
    sub_pos = jnp.where(sub < HALF, first, second) * HALF + sub % HALF
    crossing = (sub_pos >= pair_start) & (sub_pos < second_start) & (lane_pos >= second_start)
    allowed = (sub_pos <= lane_pos) & jnp.logical_not(crossing)
    diag[0] = jnp.where(allowed, 0.0, MASKED * LOG2E_SCALE)
    diag[1] = jnp.zeros((TOK, TOK), F32)
    hidden = ((sub < 64) & (sub > lane_block)) | ((sub == 64) & (lane_pos >= second_start))
    q_feat = jnp.where(hidden, MASKED, 0.0).astype(BF)

    half_lane = lax.broadcasted_iota(jnp.int32, (HALF, TOK), 1)
    half_sub = lax.broadcasted_iota(jnp.int32, (HALF, TOK), 0)

    def features(n, carry):
        p, s, r = n // 16, n // 4 % 4, n % 4
        a = (me.a - r + 4) % 4
        b = (me.b - s + 4) % 4
        x = a + me.core * (b - a)
        y = b + me.core * (a - b)
        owner = (x * 2 + (me.z // 8 + p) % 2) * 4 + y
        for h in range(2):
            which = order_ref[2 * owner + h]
            pos = which * HALF + half_sub
            inside = (pos >= pair_start) & (pos < second_start) & (half_lane == 64)
            value = jnp.where((half_lane == which) | inside, 1.0, 0.0).astype(BF)
            feat[p, s, r, h * HALF : (h + 1) * HALF] = value
        return carry

    lax.fori_loop(0, 32, features, 0)
    feat[0, 0, 0] = jnp.zeros((TOK, TOK), BF)

    q_copy.wait()
    g_copy.wait()
    weight = jnp.broadcast_to(w_ref[...].astype(F32) * (1.0 / 16.0), (TOK, TOK)).T
    for h in range(HEADS):
        rows = slice(h * TOK, (h + 1) * TOK)
        q = q_in[:, rows]
        g = (g_in[:, rows].astype(F32) * weight).astype(BF)
        q_rows[rows, :] = q
        g_rows[rows, :] = g
        qt[0:DH, rows] = q.T
        qt[DH : 2 * DH, rows] = q_feat
        gt[:, rows] = g.T
    m_run[...] = jnp.full(m_run.shape, -1e30, F32)
    l_run[...] = jnp.zeros(l_run.shape, F32)
    d_run[...] = jnp.zeros(d_run.shape, F32)
    dq_t[...] = jnp.zeros(dq_t.shape, F32)
    sum_kv[...] = jnp.zeros(sum_kv.shape, F32)

    def first_pass(p, s, own):
        keys = kv[p, s, :, 0].reshape(UNIT, DH)
        vals = kv[p, s, :, 1].reshape(UNIT, DH)
        wide = jnp.concatenate([keys, feat[p, s].reshape(UNIT, DH)], axis=1)
        scores = jnp.dot(wide, qt[...], preferred_element_type=F32) * LOG2E_SCALE
        tri = jnp.concatenate([diag[own]] * HEADS, axis=1)
        scores = jnp.concatenate([scores[0:TOK] + tri, scores[TOK:]], axis=0)
        old = m_run[...]
        new = jnp.maximum(old, jnp.max(scores, axis=0, keepdims=True))
        factor = jnp.exp2(old - new)
        e = jnp.exp2(scores - new)
        dp = jnp.dot(vals, gt[...], preferred_element_type=F32)
        l_run[...] = l_run[...] * factor + jnp.sum(e, axis=0, keepdims=True)
        d_run[...] = d_run[...] * factor + jnp.sum(e * dp, axis=0, keepdims=True)
        e_all[p, s] = e.astype(BF)
        dp_all[p, s] = dp
        m_all[p, s] = new
        m_run[...] = new
        for r in range(4):
            kt[p, s, :, r * TOK : (r + 1) * TOK] = kv[p, s, r, 0].T

    for p in range(2):
        if p == 1:
            across().wait_recv()
            open_plane(1)
        spread_plane(p)

        def first_unit(t, carry, p=p):
            s = t + t // 2 * (5 - 2 * t)

            @pl.when(t > 0)
            def _():
                for r in (0, 1, 3, 2):
                    along_b(p, s, r).wait_recv()

            first_pass(p, s, 1 if p == 1 else jnp.minimum(t, 1))
            return carry

        lax.fori_loop(0, 4, first_unit, 0)

    inverse = 1.0 / l_run[...]
    d_run[...] = d_run[...] * inverse
    l_run[...] = inverse

    def second_pass(p, s):
        share = jnp.exp2(m_all[p, s] - m_run[...]) * l_run[...]

        def tile(t, carry):
            rows = pl.ds(pl.multiple_of(t * 256, 256), 256)
            probs = e_all[p, s, rows, :].astype(F32) * share
            probs_low = probs.astype(BF)
            ds = (probs * (dp_all[p, s, rows, :] - d_run[...])).astype(BF)
            dk = jnp.dot(ds, q_rows[...], preferred_element_type=F32) * SCALE
            dv = jnp.dot(probs_low, g_rows[...], preferred_element_type=F32)
            for n in range(2):
                part[p, s, 2 * t + n, 0] = dk[n * TOK : (n + 1) * TOK].astype(BF)
                part[p, s, 2 * t + n, 1] = dv[n * TOK : (n + 1) * TOK].astype(BF)
            sum_kv[0] += jnp.sum(dk.reshape(32, 8, DH), axis=0)
            sum_kv[1] += jnp.sum(dv.reshape(32, 8, DH), axis=0)
            dq_t[...] += jnp.dot(kt[p, s, :, rows], ds, preferred_element_type=F32)
            return carry

        lax.fori_loop(0, 2, tile, 0)

    def back_b(p, s):
        return remote(
            part.at[p, s], got_b.at[p, s - 1], b_send.at[p, s - 1], b_recv.at[p, s - 1],
            me.near(0, 4 - s),
        )

    def back_a(p, r):
        return remote(
            line.at[p, r], got_a.at[p, r - 1], a_send.at[p, r - 1], a_recv.at[p, r - 1],
            me.near(4 - r, 0),
        )

    def back_z():
        return remote(fin, got_z, z_sem.at[0], z_sem.at[1], me.near(0, 0, 8))

    def second_unit(p):
        def unit(t, carry):
            s = 3 - t
            second_pass(p, s)

            @pl.when(s > 0)
            def _():
                back_b(p, s).start()

            return carry

        return unit

    def add_b(p):
        for s in (1, 2, 3):
            back_b(p, s).wait_recv()
        for r in (2, 1, 3, 0):
            total = part[p, 0, r].astype(F32)
            for s in range(3):
                total = total + got_b[p, s, r].astype(F32)
            line[p, r] = total.astype(BF)
            if r > 0:
                back_a(p, r).start()

    def add_a(p):
        total = line[p, 0].astype(F32)
        for r in (1, 3, 2):
            back_a(p, r).wait_recv()
            total = total + got_a[p, r - 1].astype(F32)
        return total

    lax.fori_loop(0, 4, second_unit(1), 0)
    lax.fori_loop(0, 2, second_unit(0), 0)
    add_b(1)
    lax.fori_loop(2, 3, second_unit(0), 0)
    fin[...] = add_a(1).astype(BF)
    back_z().start()
    lax.fori_loop(3, 4, second_unit(0), 0)

    own_sum[...] = jnp.zeros(own_sum.shape, F32)
    for h in range(HEADS):
        rows = slice(h * TOK, (h + 1) * TOK)
        dq = dq_t[:, rows].T * SCALE
        dq_ref[0, :, rows] = dq.astype(BF)
        own_sum[h : h + 1, :] = jnp.sum(dq, axis=0, keepdims=True)
    own_sum[8:9, :] = jnp.sum(sum_kv[0], axis=0, keepdims=True)
    own_sum[9:10, :] = jnp.sum(sum_kv[1], axis=0, keepdims=True)

    def plane_copy(j):
        return remote(
            own_sum, plane_sums.at[slot], plane_send.at[j], plane_recv.at[slot],
            me.in_plane((slot + j) % 16),
        )

    def plane_arrival(j):
        there = (slot + j) % 16
        return remote(
            own_sum, plane_sums.at[there], plane_send.at[j], plane_recv.at[there],
            me.in_plane(there),
        )

    def z_copy(j):
        return remote(
            plane_sum, z_sums.at[me.z], zs_send.at[j], zs_recv.at[me.z],
            me.along_z((me.z + j) % 16),
        )

    def z_arrival(j):
        there = (me.z + j) % 16
        return remote(
            plane_sum, z_sums.at[there], zs_send.at[j], zs_recv.at[there], me.along_z(there)
        )

    def core_copy():
        return remote(
            z_sum, core_sums.at[me.core], core_sem.at[0], core_sem.at[1], me.other_core()
        )

    def each(action):
        def step(j, carry):
            action(j)
            return carry

        lax.fori_loop(1, 16, step, 0)

    def added(ref, count):
        total = ref[0]
        for n in range(1, count):
            total = total + ref[n]
        return total

    each(lambda j: plane_copy(j).start())
    plane_sums[slot] = own_sum[...]
    add_b(0)
    each(lambda j: plane_arrival(j).wait_recv())
    plane_sum[...] = added(plane_sums, 16)
    each(lambda j: z_copy(j).start())
    z_sums[me.z] = plane_sum[...]
    total = add_a(0)
    dk_ref[0] = total[0].astype(BF)
    dv_ref[0] = total[1].astype(BF)
    back_z().wait_recv()
    dk_ref[0] = (total[0] + got_z[0].astype(F32)).astype(BF)
    dv_ref[0] = (total[1] + got_z[1].astype(F32)).astype(BF)
    each(lambda j: z_arrival(j).wait_recv())
    z_sum[...] = added(z_sums, 16)
    core_copy().start()
    core_sums[me.core] = z_sum[...]
    remote(
        z_sum, core_sums.at[1 - me.core], core_sem.at[0], core_sem.at[1], me.other_core()
    ).wait_recv()
    bias_ref[...] = added(core_sums, 2) * (1.0 / 256.0)

    across().wait_send()
    for p in range(2):
        for r in (1, 2, 3):
            along_a(p, r).wait_send()
            back_a(p, r).wait_send()
            back_b(p, r).wait_send()
            for s in range(4):
                along_b(p, r, s).wait_send()
    back_z().wait_send()
    each(lambda j: plane_copy(j).wait_send())
    each(lambda j: z_copy(j).wait_send())
    core_copy().wait_send()


def per_device(q_heads, k_head, v_head, out_grad, weight_codes, bounds, block_order):
    vmem = pl.BlockSpec(memory_space=pltpu.VMEM)
    smem = pl.BlockSpec(memory_space=pltpu.SMEM)
    hbm = pl.BlockSpec(memory_space=pl.ANY)
    low = lambda *shape: pltpu.VMEM(shape, BF)
    full = lambda *shape: pltpu.VMEM(shape, F32)
    dma = lambda *shape: pltpu.SemaphoreType.DMA(shape)
    scratch = [
        low(TOK, ROWS), low(TOK, ROWS),
        low(2, 4, 4, 2, TOK, DH), low(2, 4, 4, TOK, DH),
        low(2 * DH, ROWS), low(DH, ROWS), low(ROWS, DH), low(ROWS, DH),
        low(2, 4, DH, UNIT), full(2, TOK, TOK),
        low(2, 4, UNIT, ROWS), full(2, 4, UNIT, ROWS), full(2, 4, 1, ROWS),
        full(1, ROWS), full(1, ROWS), full(1, ROWS), full(DH, ROWS),
        low(2, 4, 4, 2, TOK, DH), low(2, 3, 4, 2, TOK, DH), low(2, 4, 2, TOK, DH),
        low(2, 3, 2, TOK, DH), low(2, TOK, DH), low(2, TOK, DH), full(2, 8, DH),
        full(16, DH), full(16, 16, DH), full(16, DH), full(16, 16, DH), full(16, DH),
        full(2, 16, DH),
        dma(2), dma(2, 4, 4), dma(2, 4, 4), dma(2, 3), dma(2, 3), dma(2, 3), dma(2, 3), dma(2),
        dma(16), dma(16), dma(16), dma(16), dma(2),
    ]
    dq, dk, dv, bias = pl.pallas_call(
        kernel,
        out_shape=(
            jax.ShapeDtypeStruct((1, TOK, ROWS), BF),
            jax.ShapeDtypeStruct((1, TOK, DH), BF),
            jax.ShapeDtypeStruct((1, TOK, DH), BF),
            jax.ShapeDtypeStruct((16, DH), F32),
        ),
        in_specs=[hbm, vmem, vmem, hbm, vmem, smem, smem],
        out_specs=(vmem, vmem, vmem, vmem),
        scratch_shapes=scratch,
        compiler_params=pltpu.CompilerParams(
            collective_id=0, has_side_effects=True, vmem_limit_bytes=56 * 2**20
        ),
    )(q_heads, k_head, v_head, out_grad, weight_codes, bounds, block_order)
    return dq, dk, dv, bias[:10].reshape(1280)


def solution(mesh):
    return jax.shard_map(
        per_device,
        mesh=mesh,
        in_specs=(
            P("outer", "inner", None),
            P("outer", "inner", None),
            P("outer", "inner", None),
            P("outer", "inner", None),
            P("outer", "inner"),
            P("outer", None),
            P(),
        ),
        out_specs=(
            P("outer", "inner", None),
            P("outer", "inner", None),
            P("outer", "inner", None),
            P(),
        ),
        check_vma=False,
    )
```

```python
import functools
import math

import jax
import jax.numpy as jnp
from jax import lax
from jax.experimental import pallas as pl
from jax.experimental.pallas import tpu as pltpu
from jax.sharding import PartitionSpec as P

MESH = pl.DeviceIdType.MESH
BF = jnp.bfloat16
F32 = jnp.float32
HEADS = 8
DH = 128
TOK = 128
HALF = 64
ROWS = HEADS * TOK
UNIT = 4 * TOK
SCALE = 1.0 / math.sqrt(DH)
LOG2E_SCALE = math.log2(math.e) / math.sqrt(DH)
MASKED = -(2.0**99)


class Place:
    def __init__(self):
        outer = lax.axis_index("outer")
        inner = lax.axis_index("inner")
        self.inner = inner
        self.core = outer % 2
        self.x = inner // 8
        self.y = inner % 4
        self.z = (inner // 4) % 2 * 8 + outer // 2
        self.a = self.x + self.core * (self.y - self.x)
        self.b = self.y + self.core * (self.x - self.y)

    def at(self, x, y, z, core):
        return (z % 8 * 2 + core, (x * 2 + z // 8) * 4 + y)

    def near(self, da, db, dz=0):
        a = (self.a + da) % 4
        b = (self.b + db) % 4
        x = a + self.core * (b - a)
        y = b + self.core * (a - b)
        return self.at(x, y, (self.z + dz) % 16, self.core)

    def in_plane(self, slot, core):
        return self.at(slot // 4, slot % 4, self.z, core)

    def along_z(self, z):
        return self.at(self.x, self.y, z, self.core)


def remote(src, dst, send_sem, recv_sem, device):
    return pltpu.make_async_remote_copy(
        src_ref=src,
        dst_ref=dst,
        send_sem=send_sem,
        recv_sem=recv_sem,
        device_id=device,
        device_id_type=MESH,
    )


def kernel(
    q_hbm, k_hbm, v_hbm, g_hbm, w_hbm, bounds_hbm, order_hbm,
    dq_ref, dk_ref, dv_ref, bias_ref,
    q_in, k_in, v_in, g_in, w_in, bounds_ref, order_ref,
    kv, feat, q_wide, q_t, g_rows, g_t, keys, diag,
    e_all, dp_all, m_all, m_run, l_run, d_run, dq_all,
    part, got_b, line, got_a, fin, got_z, sum_kv, dq_out, kv_total, kv_out,
    own_sum, plane_rows, row_sum, z_rows, all_rows,
    in_sem, out_sem, gather_send, gather_recv, b_send, b_recv, a_send, a_recv, z_sem,
    plane_send, plane_recv, zs_send, zs_recv, last_send, last_recv,
):
    me = Place()
    slot = me.x * 4 + me.y
    arrays = (
        (k_hbm.at[0], k_in), (v_hbm.at[0], v_in), (bounds_hbm, bounds_ref),
        (order_hbm, order_ref), (w_hbm, w_in), (q_hbm.at[0], q_in), (g_hbm.at[0], g_in),
    )
    loads = [
        pltpu.make_async_copy(source, target, in_sem.at[n])
        for n, (source, target) in enumerate(arrays)
    ]
    for load in loads:
        load.start()

    barrier = pltpu.get_barrier_semaphore()

    def greet(j, carry):
        there = (slot + j) % 16
        for device in (
            me.along_z((me.z + j) % 16), me.in_plane(there, me.core), me.in_plane(there, 1 - me.core)
        ):
            pl.semaphore_signal(barrier, inc=1, device_id=device, device_id_type=MESH)
        return carry

    pl.semaphore_signal(
        barrier, inc=1, device_id=me.in_plane(slot, 1 - me.core), device_id_type=MESH
    )
    lax.fori_loop(1, 16, greet, 0)
    for load in loads[:4]:
        load.wait()
    kv[0, 0, 0, 0] = k_in[...].T
    kv[0, 0, 0, 1] = v_in[...].T

    pair_start = bounds_ref[0, 0]
    second_start = bounds_ref[0, 1]
    lane = lax.broadcasted_iota(jnp.int32, (TOK, TOK), 1)
    sub = lax.broadcasted_iota(jnp.int32, (TOK, TOK), 0)
    first = order_ref[2 * me.inner]
    second = order_ref[2 * me.inner + 1]
    sub_block = jnp.where(sub < HALF, first, second)
    sub_pos = sub_block * HALF + sub % HALF
    lane_pos = jnp.where(lane < HALF, first, second) * HALF + lane % HALF
    crossing = (lane_pos >= pair_start) & (lane_pos < second_start) & (sub_pos >= second_start)
    allowed = (lane_pos <= sub_pos) & jnp.logical_not(crossing)
    diag[0] = jnp.where(allowed, 0.0, MASKED * LOG2E_SCALE)
    diag[1] = jnp.zeros((TOK, TOK), F32)
    hidden = ((lane < 64) & (lane > sub_block)) | ((lane == 64) & (sub_pos >= second_start))
    q_feat = jnp.where(hidden, MASKED, 0.0).astype(BF)

    def features(n, carry):
        p, s, r = n // 16, n // 4 % 4, n % 4
        a = (me.a - r + 4) % 4
        b = (me.b - s + 4) % 4
        x = a + me.core * (b - a)
        y = b + me.core * (a - b)
        owner = (x * 2 + (me.z // 8 + p) % 2) * 4 + y
        which = jnp.where(lane < HALF, order_ref[2 * owner], order_ref[2 * owner + 1])
        pos = which * HALF + lane % HALF
        inside = (pos >= pair_start) & (pos < second_start) & (sub == 64)
        feat[p, s, r] = jnp.where((sub == which) | inside, 1.0, 0.0).astype(BF)
        return carry

    lax.fori_loop(0, 32, features, 0)
    feat[0, 0, 0] = jnp.zeros((TOK, TOK), BF)

    pl.semaphore_wait(barrier, 46)

    def block(p, s, r, source, device):
        return remote(
            kv.at[source], kv.at[p, s, r], gather_send.at[p, s, r], gather_recv.at[p, s, r], device
        )

    def along_a(p, r):
        return block(p, 0, r, (p, 0, 0), me.near(r, 0))

    def along_b(p, s, r):
        return block(p, s, r, (p, 0, r), me.near(0, s))

    def across():
        return block(1, 0, 0, (0, 0, 0), me.near(0, 0, 8))

    def open_plane(p):
        for r in (2, 1, 3):
            along_a(p, r).start()
        for s in (2, 1, 3):
            along_b(p, s, 0).start()

    def pass_on(p, r):
        along_a(p, r).wait_recv()
        for s in (2, 1, 3):
            along_b(p, s, r).start()

    across().start()
    open_plane(0)

    for load in loads[4:]:
        load.wait()
    weight = jnp.broadcast_to(w_in[...].astype(F32) * (1.0 / 16.0), (TOK, TOK)).T
    for h in range(HEADS):
        rows = slice(h * TOK, (h + 1) * TOK)
        q = q_in[:, rows]
        g = (g_in[:, rows].astype(F32) * weight).astype(BF)
        q_wide[rows, 0:DH] = q
        q_wide[rows, DH : 2 * DH] = q_feat
        q_t[:, rows] = q.T
        g_rows[rows, :] = g
        g_t[:, rows] = g.T
    m_run[...] = jnp.full(m_run.shape, -1e30, F32)
    l_run[...] = jnp.zeros(l_run.shape, F32)
    d_run[...] = jnp.zeros(d_run.shape, F32)
    dq_all[...] = jnp.zeros(dq_all.shape, F32)
    sum_kv[...] = jnp.zeros(sum_kv.shape, F32)

    def first_pass(p, s, own):
        wide = jnp.concatenate(
            [
                jnp.concatenate([kv[p, s, r, 0] for r in range(4)], axis=1),
                jnp.concatenate([feat[p, s, r] for r in range(4)], axis=1),
            ],
            axis=0,
        )
        scores = jnp.dot(q_wide[...], wide, preferred_element_type=F32) * LOG2E_SCALE
        vals = jnp.concatenate([kv[p, s, r, 1] for r in range(4)], axis=1)
        dp = jnp.dot(g_rows[...], vals, preferred_element_type=F32)
        tri = jnp.concatenate([diag[own]] * HEADS, axis=0)
        blocks = [scores[:, r * TOK : (r + 1) * TOK] for r in range(4)]
        blocks[0] = blocks[0] + tri
        old = m_run[...]
        new = old
        for r in range(4):
            new = jnp.maximum(new, blocks[r])
        factor = jnp.exp2(old - new)
        l_new = l_run[...] * factor
        d_new = d_run[...] * factor
        for r in range(4):
            e = jnp.exp2(blocks[r] - new)
            dp_r = dp[:, r * TOK : (r + 1) * TOK]
            l_new = l_new + e
            d_new = d_new + e * dp_r
            e_all[p, s, r] = e.astype(BF)
            dp_all[p, s, r] = dp_r
        l_run[...] = l_new
        d_run[...] = d_new
        m_all[p, s] = new
        m_run[...] = new
        for r in range(4):
            keys[p, s, r * TOK : (r + 1) * TOK, :] = kv[p, s, r, 0].T

    for r in (1, 3, 2):
        pass_on(0, r)

    def first_unit(p):
        def unit(t, carry):
            s = t + t // 2 * (5 - 2 * t)

            @pl.when(t > 0)
            def _():
                if p == 0:
                    pass_on(1, s)
                for r in (0, 1, 3, 2):
                    along_b(p, s, r).wait_recv()

            first_pass(p, s, 1 if p == 1 else jnp.minimum(t, 1))

            if p == 0:

                @pl.when(t == 0)
                def _():
                    across().wait_recv()
                    open_plane(1)

            return carry

        return unit

    lax.fori_loop(0, 4, first_unit(0), 0)
    lax.fori_loop(0, 4, first_unit(1), 0)

    top = jnp.max(m_run[...], axis=1, keepdims=True)
    factor = jnp.exp2(m_run[...] - top)
    inverse = 1.0 / jnp.sum(l_run[...] * factor, axis=1, keepdims=True)
    delta = jnp.sum(d_run[...] * factor, axis=1, keepdims=True) * inverse
    m_run[...] = jnp.broadcast_to(top, m_run.shape)
    l_run[...] = jnp.broadcast_to(inverse, l_run.shape)
    d_run[...] = jnp.broadcast_to(delta, d_run.shape)

    def second_pass(p, s, with_v, with_k):
        share = jnp.exp2(m_all[p, s] - m_run[...]) * l_run[...]
        for t in range(2):
            low = []
            ds = []
            for r in (2 * t, 2 * t + 1):
                probs = e_all[p, s, r].astype(F32) * share
                if with_v:
                    low.append(probs.astype(BF))
                if with_k:
                    ds.append((probs * (dp_all[p, s, r] - d_run[...])).astype(BF))
            if with_v:
                dv = jnp.dot(g_t[...], jnp.concatenate(low, axis=1), preferred_element_type=F32)
                for n in range(2):
                    part[p, s, 1, 2 * t + n] = dv[:, n * TOK : (n + 1) * TOK].astype(BF)
                sum_kv[1] += dv[:, :TOK] + dv[:, TOK:]
            if with_k:
                ds = jnp.concatenate(ds, axis=1)
                dk = jnp.dot(q_t[...], ds, preferred_element_type=F32) * SCALE
                for n in range(2):
                    part[p, s, 0, 2 * t + n] = dk[:, n * TOK : (n + 1) * TOK].astype(BF)
                sum_kv[0] += dk[:, :TOK] + dk[:, TOK:]
                dq_all[...] += jnp.dot(
                    ds, keys[p, s, 256 * t : 256 * t + 256, :], preferred_element_type=F32
                )

    def back_b(p, s, v):
        return remote(
            part.at[p, s, v], got_b.at[p, s - 1, v], b_send.at[p, s - 1, v],
            b_recv.at[p, s - 1, v], me.near(0, 4 - s),
        )

    def back_a(p, r, v):
        return remote(
            line.at[p, r, v], got_a.at[p, r - 1, v], a_send.at[p, r - 1, v],
            a_recv.at[p, r - 1, v], me.near(4 - r, 0),
        )

    def back_z(v):
        return remote(fin.at[v], got_z.at[v], z_sem.at[v, 0], z_sem.at[v, 1], me.near(0, 0, 8))

    def far_unit(v):
        def unit(t, carry):
            s = 3 - t
            second_pass(1, s, v == 1, v == 0)

            @pl.when(s > 0)
            def _():
                back_b(1, s, v).start()

            return carry

        return unit

    def near_unit(t, carry):
        second_pass(0, 3 - t, True, True)
        return carry

    def add_b(p, v):
        for s in (3, 2, 1):
            back_b(p, s, v).wait_recv()
        for r in (2, 1, 3, 0):
            total = part[p, 0, v, r].astype(F32)
            for s in range(3):
                total = total + got_b[p, s, v, r].astype(F32)
            line[p, r, v] = total.astype(BF)
            if r > 0:
                back_a(p, r, v).start()

    def add_a(p, v):
        total = line[p, 0, v].astype(F32)
        for r in (1, 3, 2):
            back_a(p, r, v).wait_recv()
            total = total + got_a[p, r - 1, v].astype(F32)
        return total

    lax.fori_loop(0, 4, far_unit(1), 0)
    lax.fori_loop(0, 4, far_unit(0), 0)
    lax.fori_loop(0, 2, near_unit, 0)
    add_b(1, 1)
    back_b(0, 2, 1).start()
    back_b(0, 2, 0).start()
    lax.fori_loop(2, 4, near_unit, 0)

    for h in range(HEADS):
        rows = slice(h * TOK, (h + 1) * TOK)
        dq = dq_all[rows, :] * SCALE
        dq_out[:, rows] = dq.astype(BF)
        own_sum[h] = jnp.sum(dq, axis=0, keepdims=True)
    own_sum[8] = jnp.sum(sum_kv[0].T, axis=0, keepdims=True)
    own_sum[9] = jnp.sum(sum_kv[1].T, axis=0, keepdims=True)
    number = me.core * 16 + slot
    adds = (slot < 10) & (me.core == slot % 2)

    def plane_copy(j):
        return remote(
            own_sum.at[j], plane_rows.at[number], plane_send.at[j], plane_recv.at[number],
            me.in_plane(j, j % 2),
        )

    def plane_arrival(j):
        there = (number + j) % 32
        return remote(
            own_sum.at[0], plane_rows.at[there], plane_send.at[0], plane_recv.at[there],
            me.in_plane(there % 16, there // 16),
        )

    def z_copy(j):
        return remote(
            row_sum, z_rows.at[me.z], zs_send.at[j], zs_recv.at[me.z],
            me.along_z((me.z + j) % 16),
        )

    def z_arrival(j):
        there = (me.z + j) % 16
        return remote(
            row_sum, z_rows.at[there], zs_send.at[j], zs_recv.at[there], me.along_z(there)
        )

    def last_copy(j):
        there = (number + j) % 32
        return remote(
            all_rows.at[slot], all_rows.at[slot], last_send.at[j], last_recv.at[slot],
            me.in_plane(there % 16, there // 16),
        )

    def last_arrival(j):
        return remote(
            all_rows.at[j], all_rows.at[j], last_send.at[0], last_recv.at[j],
            me.in_plane(j, j % 2),
        )

    def each(start, stop, action):
        def step(j, carry):
            action(j)
            return carry

        lax.fori_loop(start, stop, step, 0)

    def each_row(action):
        def unless_mine(j):
            @pl.when(jnp.logical_not((slot == j) & (me.core == j % 2)))
            def _():
                action(j)

        each(0, 10, unless_mine)

    def added(ref, count):
        total = ref[0]
        for n in range(1, count):
            total = total + ref[n]
        return total

    each_row(lambda j: plane_copy(j).start())
    add_b(1, 0)
    for v in (1, 0):
        back_b(0, 1, v).start()
        back_b(0, 3, v).start()
    fin[1] = add_a(1, 1).astype(BF)
    back_z(1).start()
    dq_copy = pltpu.make_async_copy(dq_out, dq_ref.at[0], out_sem.at[0])
    dq_copy.start()

    @pl.when(adds)
    def _():
        plane_rows[number] = own_sum[slot]
        each(1, 32, lambda j: plane_arrival(j).wait_recv())
        row_sum[...] = added(plane_rows, 32)
        each(1, 16, lambda j: z_copy(j).start())
        z_rows[me.z] = row_sum[...]

    fin[0] = add_a(1, 0).astype(BF)
    back_z(0).start()
    add_b(0, 1)
    add_b(0, 0)

    @pl.when(adds)
    def _():
        each(1, 16, lambda j: z_arrival(j).wait_recv())
        all_rows[slot] = added(z_rows, 16) * (1.0 / 256.0)
        each(1, 32, lambda j: last_copy(j).start())

    kv_total[1] = add_a(0, 1)
    kv_total[0] = add_a(0, 0)
    for v in (1, 0):
        back_z(v).wait_recv()
        kv_out[v] = (kv_total[v] + got_z[v].astype(F32)).T.astype(BF)
    dk_copy = pltpu.make_async_copy(kv_out.at[0], dk_ref.at[0], out_sem.at[1])
    dv_copy = pltpu.make_async_copy(kv_out.at[1], dv_ref.at[0], out_sem.at[2])
    dk_copy.start()
    dv_copy.start()
    each_row(lambda j: last_arrival(j).wait_recv())
    for n in range(10):
        bias_ref[n] = all_rows[n]
    dq_copy.wait()
    dk_copy.wait()
    dv_copy.wait()

    across().wait_send()
    for p in range(2):
        for r in (1, 2, 3):
            along_a(p, r).wait_send()
            for v in range(2):
                back_a(p, r, v).wait_send()
                back_b(p, r, v).wait_send()
            for s in range(4):
                along_b(p, r, s).wait_send()
    for v in range(2):
        back_z(v).wait_send()
    each_row(lambda j: plane_copy(j).wait_send())

    @pl.when(adds)
    def _():
        each(1, 16, lambda j: z_copy(j).wait_send())
        each(1, 32, lambda j: last_copy(j).wait_send())


def deliver(dq_in, dk_in, dv_in, bias_in, dq_ref, dk_ref, dv_ref, bias_ref):
    dq_ref[...] = dq_in[...]
    dk_ref[...] = dk_in[...]
    dv_ref[...] = dv_in[...]
    for n in range(10):
        bias_ref[n * DH : (n + 1) * DH] = bias_in[n, 0]


def per_device(q_heads, k_head, v_head, out_grad, weight_codes, bounds, block_order):
    vmem = pl.BlockSpec(memory_space=pltpu.VMEM)
    hbm = pl.BlockSpec(memory_space=pl.ANY)
    low = lambda *shape: pltpu.VMEM(shape, BF)
    full = lambda *shape: pltpu.VMEM(shape, F32)
    dma = lambda *shape: pltpu.SemaphoreType.DMA(shape)
    scratch = [
        low(TOK, ROWS), low(TOK, DH), low(TOK, DH), low(TOK, ROWS),
        pltpu.VMEM((1, TOK), jnp.int32), pltpu.SMEM((1, 2), jnp.int32), pltpu.SMEM((64,), jnp.int32),
        low(2, 4, 4, 2, DH, TOK), low(2, 4, 4, TOK, TOK),
        low(ROWS, 2 * DH), low(DH, ROWS), low(ROWS, DH), low(DH, ROWS),
        low(2, 4, UNIT, DH), full(2, TOK, TOK),
        low(2, 4, 4, ROWS, TOK), full(2, 4, 4, ROWS, TOK), full(2, 4, ROWS, TOK),
        full(ROWS, TOK), full(ROWS, TOK), full(ROWS, TOK), full(ROWS, DH),
        low(2, 4, 2, 4, DH, TOK), low(2, 3, 2, 4, DH, TOK), low(2, 4, 2, DH, TOK),
        low(2, 3, 2, DH, TOK), low(2, DH, TOK), low(2, DH, TOK), full(2, DH, TOK),
        low(TOK, ROWS), full(2, DH, TOK), low(2, TOK, DH),
        full(10, 1, DH), full(32, 1, DH), full(1, DH), full(16, 1, DH), full(10, 1, DH),
        dma(7), dma(3), dma(2, 4, 4), dma(2, 4, 4), dma(2, 3, 2), dma(2, 3, 2), dma(2, 3, 2),
        dma(2, 3, 2), dma(2, 2), dma(10), dma(32), dma(16), dma(16), dma(32), dma(10),
    ]
    dq, dk, dv, bias = pl.pallas_call(
        kernel,
        out_shape=(
            jax.ShapeDtypeStruct((1, TOK, ROWS), BF),
            jax.ShapeDtypeStruct((1, TOK, DH), BF),
            jax.ShapeDtypeStruct((1, TOK, DH), BF),
            jax.ShapeDtypeStruct((10, 1, DH), F32),
        ),
        in_specs=[hbm] * 7,
        out_specs=(hbm, hbm, hbm, vmem),
        scratch_shapes=scratch,
        compiler_params=pltpu.CompilerParams(
            collective_id=0, has_side_effects=True, vmem_limit_bytes=56 * 2**20
        ),
    )(q_heads, k_head, v_head, out_grad, weight_codes, bounds, block_order)
    return pl.pallas_call(
        deliver,
        out_shape=(
            jax.ShapeDtypeStruct((1, TOK, ROWS), BF),
            jax.ShapeDtypeStruct((1, TOK, DH), BF),
            jax.ShapeDtypeStruct((1, TOK, DH), BF),
            jax.ShapeDtypeStruct((1280,), F32),
        ),
        in_specs=[vmem] * 4,
        out_specs=(vmem,) * 4,
    )(dq, dk, dv, bias)


def solution(mesh):
    return jax.shard_map(
        per_device,
        mesh=mesh,
        in_specs=(
            P("outer", "inner", None),
            P("outer", "inner", None),
            P("outer", "inner", None),
            P("outer", "inner", None),
            P("outer", "inner"),
            P("outer", None),
            P(),
        ),
        out_specs=(
            P("outer", "inner", None),
            P("outer", "inner", None),
            P("outer", "inner", None),
            P(),
        ),
        check_vma=False,
    )
```

```python
import functools
import math

import jax
import jax.numpy as jnp
from jax import lax
from jax.experimental import pallas as pl
from jax.experimental.pallas import tpu as pltpu
from jax.sharding import PartitionSpec as P

MESH = pl.DeviceIdType.MESH
BF = jnp.bfloat16
F32 = jnp.float32
HEADS = 8
DH = 128
TOK = 128
HALF = 64
ROWS = HEADS * TOK
UNIT = 4 * TOK
SCALE = 1.0 / math.sqrt(DH)
LOG2E_SCALE = math.log2(math.e) / math.sqrt(DH)
MASKED = -(2.0**99)


class Place:
    def __init__(self):
        outer = lax.axis_index("outer")
        inner = lax.axis_index("inner")
        self.inner = inner
        self.core = outer % 2
        self.x = inner // 8
        self.y = inner % 4
        self.z = (inner // 4) % 2 * 8 + outer // 2
        self.a = self.x + self.core * (self.y - self.x)
        self.b = self.y + self.core * (self.x - self.y)

    def at(self, x, y, z, core):
        return (z % 8 * 2 + core, (x * 2 + z // 8) * 4 + y)

    def near(self, da, db, dz=0):
        a = (self.a + da) % 4
        b = (self.b + db) % 4
        x = a + self.core * (b - a)
        y = b + self.core * (a - b)
        return self.at(x, y, (self.z + dz) % 16, self.core)

    def in_plane(self, slot, core):
        return self.at(slot // 4, slot % 4, self.z, core)

    def along_z(self, z):
        return self.at(self.x, self.y, z, self.core)


def remote(src, dst, send_sem, recv_sem, device):
    return pltpu.make_async_remote_copy(
        src_ref=src,
        dst_ref=dst,
        send_sem=send_sem,
        recv_sem=recv_sem,
        device_id=device,
        device_id_type=MESH,
    )


def kernel(
    q_hbm, k_hbm, v_hbm, g_hbm, w_hbm, bounds_hbm, order_hbm,
    dq_ref, dk_ref, dv_ref, bias_ref,
    q_in, k_in, v_in, g_in, w_in, bounds_ref, order_ref,
    kv, feat, q_wide, q_t, g_rows, g_t, keys, diag,
    e_all, dp_all, m_all, m_run, l_run, d_run, dq_all,
    part, got_b, line, got_a, fin, got_z, sum_kv, dq_out, kv_total, kv_out,
    own_sum, plane_rows, row_sum, z_rows, all_rows,
    in_sem, out_sem, gather_send, gather_recv, b_send, b_recv, a_send, a_recv, z_sem,
    plane_send, plane_recv, zs_send, zs_recv, last_send, last_recv,
):
    me = Place()
    slot = me.x * 4 + me.y
    arrays = (
        (k_hbm.at[0], k_in), (v_hbm.at[0], v_in), (bounds_hbm, bounds_ref),
        (order_hbm, order_ref), (w_hbm, w_in), (q_hbm.at[0], q_in), (g_hbm.at[0], g_in),
    )
    loads = [
        pltpu.make_async_copy(source, target, in_sem.at[n])
        for n, (source, target) in enumerate(arrays)
    ]
    for load in loads:
        load.start()

    barrier = pltpu.get_barrier_semaphore()

    def greet(j, carry):
        there = (slot + j) % 16
        for device in (
            me.along_z((me.z + j) % 16), me.in_plane(there, me.core), me.in_plane(there, 1 - me.core)
        ):
            pl.semaphore_signal(barrier, inc=1, device_id=device, device_id_type=MESH)
        return carry

    pl.semaphore_signal(
        barrier, inc=1, device_id=me.in_plane(slot, 1 - me.core), device_id_type=MESH
    )
    lax.fori_loop(1, 16, greet, 0)
    for load in loads[:4]:
        load.wait()
    kv[0, 0, 0, 0] = k_in[...].T
    kv[0, 0, 0, 1] = v_in[...].T

    pair_start = bounds_ref[0, 0]
    second_start = bounds_ref[0, 1]
    lane = lax.broadcasted_iota(jnp.int32, (TOK, TOK), 1)
    sub = lax.broadcasted_iota(jnp.int32, (TOK, TOK), 0)
    first = order_ref[2 * me.inner]
    second = order_ref[2 * me.inner + 1]
    sub_block = jnp.where(sub < HALF, first, second)
    sub_pos = sub_block * HALF + sub % HALF
    lane_pos = jnp.where(lane < HALF, first, second) * HALF + lane % HALF
    crossing = (lane_pos >= pair_start) & (lane_pos < second_start) & (sub_pos >= second_start)
    allowed = (lane_pos <= sub_pos) & jnp.logical_not(crossing)
    diag[0] = jnp.where(allowed, 0.0, MASKED * LOG2E_SCALE)
    diag[1] = jnp.zeros((TOK, TOK), F32)
    hidden = ((lane < 64) & (lane > sub_block)) | ((lane == 64) & (sub_pos >= second_start))
    q_feat = jnp.where(hidden, MASKED, 0.0).astype(BF)

    def features(n, carry):
        p, s, r = n // 16, n // 4 % 4, n % 4
        a = (me.a - r + 4) % 4
        b = (me.b - s + 4) % 4
        x = a + me.core * (b - a)
        y = b + me.core * (a - b)
        owner = (x * 2 + (me.z // 8 + p) % 2) * 4 + y
        which = jnp.where(lane < HALF, order_ref[2 * owner], order_ref[2 * owner + 1])
        pos = which * HALF + lane % HALF
        inside = (pos >= pair_start) & (pos < second_start) & (sub == 64)
        feat[p, s, r] = jnp.where((sub == which) | inside, 1.0, 0.0).astype(BF)
        return carry

    lax.fori_loop(0, 32, features, 0)
    feat[0, 0, 0] = jnp.zeros((TOK, TOK), BF)

    pl.semaphore_wait(barrier, 46)

    pieces = ((None,), (0, 1))

    def block(p, s, r, v, source, device):
        at = (source, (p, s, r)) if v is None else (source + (v,), (p, s, r, v))
        sem = (p, s, r, 0 if v is None else v)
        return remote(
            kv.at[at[0]], kv.at[at[1]], gather_send.at[sem], gather_recv.at[sem], device
        )

    def along_a(p, r, v):
        return block(p, 0, r, v, (p, 0, 0), me.near(r, 0))

    def along_b(p, s, r, v):
        return block(p, s, r, v, (p, 0, r), me.near(0, s))

    def across(v):
        return block(1, 0, 0, v, (0, 0, 0), me.near(0, 0, 8))

    def open_plane(p, v):
        for r in (2, 1, 3):
            along_a(p, r, v).start()
        for s in (2, 1, 3):
            along_b(p, s, 0, v).start()

    def pass_on(p, r):
        for v in pieces[p]:
            along_a(p, r, v).wait_recv()
            for s in (2, 1, 3):
                along_b(p, s, r, v).start()

    for v in pieces[1]:
        across(v).start()
    open_plane(0, None)

    for load in loads[4:]:
        load.wait()
    weight = jnp.broadcast_to(w_in[...].astype(F32) * (1.0 / 16.0), (TOK, TOK)).T
    for h in range(HEADS):
        rows = slice(h * TOK, (h + 1) * TOK)
        q = q_in[:, rows]
        g = (g_in[:, rows].astype(F32) * weight).astype(BF)
        q_wide[rows, 0:DH] = q
        q_wide[rows, DH : 2 * DH] = q_feat
        q_t[:, rows] = q.T
        g_rows[rows, :] = g
        g_t[:, rows] = g.T
    m_run[...] = jnp.full(m_run.shape, -1e30, F32)
    l_run[...] = jnp.zeros(l_run.shape, F32)
    d_run[...] = jnp.zeros(d_run.shape, F32)
    dq_all[...] = jnp.zeros(dq_all.shape, F32)
    sum_kv[...] = jnp.zeros(sum_kv.shape, F32)

    def first_pass(p, s, own):
        wide = jnp.concatenate(
            [
                jnp.concatenate([kv[p, s, r, 0] for r in range(4)], axis=1),
                jnp.concatenate([feat[p, s, r] for r in range(4)], axis=1),
            ],
            axis=0,
        )
        scores = jnp.dot(q_wide[...], wide, preferred_element_type=F32) * LOG2E_SCALE
        vals = jnp.concatenate([kv[p, s, r, 1] for r in range(4)], axis=1)
        dp = jnp.dot(g_rows[...], vals, preferred_element_type=F32)
        tri = jnp.concatenate([diag[own]] * HEADS, axis=0)
        blocks = [scores[:, r * TOK : (r + 1) * TOK] for r in range(4)]
        blocks[0] = blocks[0] + tri
        old = m_run[...]
        new = old
        for r in range(4):
            new = jnp.maximum(new, blocks[r])
        factor = jnp.exp2(old - new)
        l_new = l_run[...] * factor
        d_new = d_run[...] * factor
        for r in range(4):
            e = jnp.exp2(blocks[r] - new)
            dp_r = dp[:, r * TOK : (r + 1) * TOK]
            l_new = l_new + e
            d_new = d_new + e * dp_r
            e_all[p, s, r] = e.astype(BF)
            dp_all[p, s, r] = dp_r
        l_run[...] = l_new
        d_run[...] = d_new
        m_all[p, s] = new
        m_run[...] = new
        for r in range(4):
            keys[p, s, r * TOK : (r + 1) * TOK, :] = kv[p, s, r, 0].T

    for r in (1, 3, 2):
        pass_on(0, r)

    def first_unit(p):
        def unit(t, carry):
            s = t + t // 2 * (5 - 2 * t)

            @pl.when(t > 0)
            def _():
                if p == 0:
                    pass_on(1, s)
                for r in (0, 1, 3, 2):
                    for v in pieces[p]:
                        along_b(p, s, r, v).wait_recv()

            first_pass(p, s, 1 if p == 1 else jnp.minimum(t, 1))

            if p == 0:

                @pl.when(t == 0)
                def _():
                    for v in pieces[1]:
                        across(v).wait_recv()
                        open_plane(1, v)

            return carry

        return unit

    lax.fori_loop(0, 4, first_unit(0), 0)
    lax.fori_loop(0, 4, first_unit(1), 0)

    top = jnp.max(m_run[...], axis=1, keepdims=True)
    factor = jnp.exp2(m_run[...] - top)
    inverse = 1.0 / jnp.sum(l_run[...] * factor, axis=1, keepdims=True)
    delta = jnp.sum(d_run[...] * factor, axis=1, keepdims=True) * inverse
    m_run[...] = jnp.broadcast_to(top, m_run.shape)
    l_run[...] = jnp.broadcast_to(inverse, l_run.shape)
    d_run[...] = jnp.broadcast_to(delta, d_run.shape)

    def second_pass(p, s, with_v, with_k):
        if with_v:
            share = jnp.exp2(m_all[p, s] - m_run[...]) * l_run[...]
        for t in range(2):
            low = []
            ds = []
            for r in (2 * t, 2 * t + 1):
                probs = e_all[p, s, r].astype(F32)
                if with_v:
                    probs = probs * share
                    low.append(probs.astype(BF))
                    if not with_k:
                        e_all[p, s, r] = low[-1]
                if with_k:
                    ds.append((probs * (dp_all[p, s, r] - d_run[...])).astype(BF))
            if with_v:
                dv = jnp.dot(g_t[...], jnp.concatenate(low, axis=1), preferred_element_type=F32)
                for n in range(2):
                    part[p, s, 1, 2 * t + n] = dv[:, n * TOK : (n + 1) * TOK].astype(BF)
                sum_kv[1] += dv[:, :TOK] + dv[:, TOK:]
            if with_k:
                ds = jnp.concatenate(ds, axis=1)
                dk = jnp.dot(q_t[...], ds, preferred_element_type=F32) * SCALE
                for n in range(2):
                    part[p, s, 0, 2 * t + n] = dk[:, n * TOK : (n + 1) * TOK].astype(BF)
                sum_kv[0] += dk[:, :TOK] + dk[:, TOK:]
                dq_all[...] += jnp.dot(
                    ds, keys[p, s, 256 * t : 256 * t + 256, :], preferred_element_type=F32
                )

    def back_b(p, s, v):
        return remote(
            part.at[p, s, v], got_b.at[p, s - 1, v], b_send.at[p, s - 1, v],
            b_recv.at[p, s - 1, v], me.near(0, 4 - s),
        )

    def back_a(p, r, v):
        return remote(
            line.at[p, r, v], got_a.at[p, r - 1, v], a_send.at[p, r - 1, v],
            a_recv.at[p, r - 1, v], me.near(4 - r, 0),
        )

    def back_z(v):
        return remote(fin.at[v], got_z.at[v], z_sem.at[v, 0], z_sem.at[v, 1], me.near(0, 0, 8))

    def far_unit(v):
        def unit(t, carry):
            s = 3 - t
            second_pass(1, s, v == 1, v == 0)

            @pl.when(s > 0)
            def _():
                back_b(1, s, v).start()

            return carry

        return unit

    def near_unit(t, carry):
        second_pass(0, 3 - t, True, True)
        return carry

    def add_b(p, v):
        for s in (3, 2, 1):
            back_b(p, s, v).wait_recv()
        for r in (2, 1, 3, 0):
            total = part[p, 0, v, r].astype(F32)
            for s in range(3):
                total = total + got_b[p, s, v, r].astype(F32)
            line[p, r, v] = total.astype(BF)
            if r > 0:
                back_a(p, r, v).start()

    def add_a(p, v):
        total = line[p, 0, v].astype(F32)
        for r in (1, 3, 2):
            back_a(p, r, v).wait_recv()
            total = total + got_a[p, r - 1, v].astype(F32)
        return total

    lax.fori_loop(0, 4, far_unit(1), 0)
    lax.fori_loop(0, 4, far_unit(0), 0)
    lax.fori_loop(0, 2, near_unit, 0)
    add_b(1, 1)
    back_b(0, 2, 1).start()
    back_b(0, 2, 0).start()
    lax.fori_loop(2, 4, near_unit, 0)

    for h in range(HEADS):
        rows = slice(h * TOK, (h + 1) * TOK)
        dq = dq_all[rows, :] * SCALE
        dq_out[:, rows] = dq.astype(BF)
        own_sum[h] = jnp.sum(dq, axis=0, keepdims=True)
    own_sum[8] = jnp.sum(sum_kv[0].T, axis=0, keepdims=True)
    own_sum[9] = jnp.sum(sum_kv[1].T, axis=0, keepdims=True)
    number = me.core * 16 + slot
    adds = (slot < 10) & (me.core == slot % 2)

    def plane_copy(j):
        return remote(
            own_sum.at[j], plane_rows.at[number], plane_send.at[j], plane_recv.at[number],
            me.in_plane(j, j % 2),
        )

    def plane_arrival(j):
        there = (number + j) % 32
        return remote(
            own_sum.at[0], plane_rows.at[there], plane_send.at[0], plane_recv.at[there],
            me.in_plane(there % 16, there // 16),
        )

    def z_copy(j):
        return remote(
            row_sum, z_rows.at[me.z], zs_send.at[j], zs_recv.at[me.z],
            me.along_z((me.z + j) % 16),
        )

    def z_arrival(j):
        there = (me.z + j) % 16
        return remote(
            row_sum, z_rows.at[there], zs_send.at[j], zs_recv.at[there], me.along_z(there)
        )

    def last_copy(j):
        there = (number + j) % 32
        return remote(
            all_rows.at[slot], all_rows.at[slot], last_send.at[j], last_recv.at[slot],
            me.in_plane(there % 16, there // 16),
        )

    def last_arrival(j):
        return remote(
            all_rows.at[j], all_rows.at[j], last_send.at[0], last_recv.at[j],
            me.in_plane(j, j % 2),
        )

    def each(start, stop, action):
        def step(j, carry):
            action(j)
            return carry

        lax.fori_loop(start, stop, step, 0)

    def each_row(action):
        def unless_mine(j):
            @pl.when(jnp.logical_not((slot == j) & (me.core == j % 2)))
            def _():
                action(j)

        each(0, 10, unless_mine)

    def added(ref, count):
        total = ref[0]
        for n in range(1, count):
            total = total + ref[n]
        return total

    each_row(lambda j: plane_copy(j).start())
    add_b(1, 0)
    for s in (1, 3):
        for v in (1, 0):
            back_b(0, s, v).start()
    fin[1] = add_a(1, 1).astype(BF)
    back_z(1).start()
    dq_copy = pltpu.make_async_copy(dq_out, dq_ref.at[0], out_sem.at[0])
    dq_copy.start()
    for v in pieces[1]:
        across(v).wait_send()
    for p in range(2):
        for r in (1, 2, 3):
            for v in pieces[p]:
                along_a(p, r, v).wait_send()
                for s in range(4):
                    along_b(p, r, s, v).wait_send()

    @pl.when(adds)
    def _():
        plane_rows[number] = own_sum[slot]
        each(1, 32, lambda j: plane_arrival(j).wait_recv())
        row_sum[...] = added(plane_rows, 32)
        each(1, 16, lambda j: z_copy(j).start())
        z_rows[me.z] = row_sum[...]

    fin[0] = add_a(1, 0).astype(BF)
    back_z(0).start()
    add_b(0, 1)
    add_b(0, 0)
    for r in (1, 2, 3):
        for v in range(2):
            back_a(1, r, v).wait_send()
            back_b(1, r, v).wait_send()

    @pl.when(adds)
    def _():
        each(1, 16, lambda j: z_arrival(j).wait_recv())
        all_rows[slot] = added(z_rows, 16) * (1.0 / 256.0)
        each(1, 32, lambda j: last_copy(j).start())

    kv_total[1] = add_a(0, 1)
    kv_total[0] = add_a(0, 0)
    for v in (1, 0):
        back_z(v).wait_recv()
        kv_out[v] = (kv_total[v] + got_z[v].astype(F32)).T.astype(BF)
    dk_copy = pltpu.make_async_copy(kv_out.at[0], dk_ref.at[0], out_sem.at[1])
    dv_copy = pltpu.make_async_copy(kv_out.at[1], dv_ref.at[0], out_sem.at[2])
    dk_copy.start()
    dv_copy.start()
    each_row(lambda j: last_arrival(j).wait_recv())
    for n in range(10):
        bias_ref[n] = all_rows[n]
    dq_copy.wait()
    dk_copy.wait()
    dv_copy.wait()

    for r in (1, 2, 3):
        for v in range(2):
            back_a(0, r, v).wait_send()
            back_b(0, r, v).wait_send()
    for v in range(2):
        back_z(v).wait_send()
    each_row(lambda j: plane_copy(j).wait_send())

    @pl.when(adds)
    def _():
        each(1, 16, lambda j: z_copy(j).wait_send())
        each(1, 32, lambda j: last_copy(j).wait_send())


def deliver(dq_in, dk_in, dv_in, bias_in, dq_ref, dk_ref, dv_ref, bias_ref):
    dq_ref[...] = dq_in[...]
    dk_ref[...] = dk_in[...]
    dv_ref[...] = dv_in[...]
    for n in range(10):
        bias_ref[n * DH : (n + 1) * DH] = bias_in[n, 0]


def per_device(q_heads, k_head, v_head, out_grad, weight_codes, bounds, block_order):
    vmem = pl.BlockSpec(memory_space=pltpu.VMEM)
    hbm = pl.BlockSpec(memory_space=pl.ANY)
    low = lambda *shape: pltpu.VMEM(shape, BF)
    full = lambda *shape: pltpu.VMEM(shape, F32)
    dma = lambda *shape: pltpu.SemaphoreType.DMA(shape)
    scratch = [
        low(TOK, ROWS), low(TOK, DH), low(TOK, DH), low(TOK, ROWS),
        pltpu.VMEM((1, TOK), jnp.int32), pltpu.SMEM((1, 2), jnp.int32), pltpu.SMEM((64,), jnp.int32),
        low(2, 4, 4, 2, DH, TOK), low(2, 4, 4, TOK, TOK),
        low(ROWS, 2 * DH), low(DH, ROWS), low(ROWS, DH), low(DH, ROWS),
        low(2, 4, UNIT, DH), full(2, TOK, TOK),
        low(2, 4, 4, ROWS, TOK), full(2, 4, 4, ROWS, TOK), full(2, 4, ROWS, TOK),
        full(ROWS, TOK), full(ROWS, TOK), full(ROWS, TOK), full(ROWS, DH),
        low(2, 4, 2, 4, DH, TOK), low(2, 3, 2, 4, DH, TOK), low(2, 4, 2, DH, TOK),
        low(2, 3, 2, DH, TOK), low(2, DH, TOK), low(2, DH, TOK), full(2, DH, TOK),
        low(TOK, ROWS), full(2, DH, TOK), low(2, TOK, DH),
        full(10, 1, DH), full(32, 1, DH), full(1, DH), full(16, 1, DH), full(10, 1, DH),
        dma(7), dma(3), dma(2, 4, 4, 2), dma(2, 4, 4, 2), dma(2, 3, 2), dma(2, 3, 2), dma(2, 3, 2),
        dma(2, 3, 2), dma(2, 2), dma(10), dma(32), dma(16), dma(16), dma(32), dma(10),
    ]
    dq, dk, dv, bias = pl.pallas_call(
        kernel,
        out_shape=(
            jax.ShapeDtypeStruct((1, TOK, ROWS), BF),
            jax.ShapeDtypeStruct((1, TOK, DH), BF),
            jax.ShapeDtypeStruct((1, TOK, DH), BF),
            jax.ShapeDtypeStruct((10, 1, DH), F32),
        ),
        in_specs=[hbm] * 7,
        out_specs=(hbm, hbm, hbm, vmem),
        scratch_shapes=scratch,
        compiler_params=pltpu.CompilerParams(
            collective_id=0, has_side_effects=True, vmem_limit_bytes=56 * 2**20
        ),
    )(q_heads, k_head, v_head, out_grad, weight_codes, bounds, block_order)
    return pl.pallas_call(
        deliver,
        out_shape=(
            jax.ShapeDtypeStruct((1, TOK, ROWS), BF),
            jax.ShapeDtypeStruct((1, TOK, DH), BF),
            jax.ShapeDtypeStruct((1, TOK, DH), BF),
            jax.ShapeDtypeStruct((1280,), F32),
        ),
        in_specs=[vmem] * 4,
        out_specs=(vmem,) * 4,
    )(dq, dk, dv, bias)


def solution(mesh):
    return jax.shard_map(
        per_device,
        mesh=mesh,
        in_specs=(
            P("outer", "inner", None),
            P("outer", "inner", None),
            P("outer", "inner", None),
            P("outer", "inner", None),
            P("outer", "inner"),
            P("outer", None),
            P(),
        ),
        out_specs=(
            P("outer", "inner", None),
            P("outer", "inner", None),
            P("outer", "inner", None),
            P(),
        ),
        check_vma=False,
    )
```
